32 devices in a mesh: groups: 1, dp: 8 (over z, y), fsdp: 4 (over x, core).
Axes of the slice: x: 2, y: 2, z: 4, core: 2. Of those that a mesh axis runs over, the one named last changes fastest.
Arguments:
- activations: bfloat16 [4096, 4096], P(('groups', 'dp', 'fsdp')), may hold values from -6 to 6
- gate_values: bfloat16 [4096, 14336], P(('groups', 'dp'), 'fsdp'), may hold values from -6 to 6
- up_values: bfloat16 [4096, 14336], P(('groups', 'dp'), 'fsdp'), may hold values from -6 to 6
- cotangent: bfloat16 [4096, 4096], P(('groups', 'dp', 'fsdp')), may hold values from -6 to 6
- down_weight: bfloat16 [14336, 4096], P('fsdp', 'dp'), may hold values from -0.09375 to 0.09375
- up_entry: bfloat16 [64, 4096], replicated, may hold values from -0.09375 to 0.09375
- up_exit: bfloat16 [64, 14336], P(None, 'fsdp'), may hold values from -0.046875 to 0.046875
- down_entry: bfloat16 [64, 14336], P(None, 'fsdp'), may hold values from -0.046875 to 0.046875
- down_exit: bfloat16 [64, 4096], replicated, may hold values from -0.09375 to 0.09375
- queries: bfloat16 [1024, 2, 4096], P('dp', None, 'fsdp'), may hold values from -0.0029296875 to 0.0029296875
- fisher: bfloat16 [2, 4096, 4096], P(None, 'fsdp', 'dp'), may hold values from -1 to 4.5, as said below
Outputs:
- scores: float32 [1024, 8], P(('dp', 'fsdp'), 'groups')
The draws below stay inside these ranges and needn't reach their ends.
Inputs may be any that keep to these rules, and one draw needn't show every extreme that they name: `fisher`: each layer's matrix is symmetric, its diagonal positive and larger than the rest of its row.
All inputs are finite; a program needn't handle non-finite values.
Results may differ from the reference program's by a relative error of at most 0.0029.
Values may be sent and summed in bfloat16 or wider, within the bound.
A program may use at most 128 MiB of HBM per device.

```python
import math
import jax
import jax.numpy as jnp
from jax import lax

D = 4096
FF = 14336
RANK = 64
LEN = 512
TOKENS = 4096
SEQS = 8
K2 = 4096
NQ = 1024


def draw_fisher(key, part):
    key = jax.random.fold_in(key, 7)
    diag_key, off_key = jax.random.split(key)
    width = RANK * RANK
    diagonal = jnp.exp(jax.random.uniform(diag_key, (2, width), jnp.float32, math.log(0.5), math.log(2.0)))
    raw = jnp.clip(jax.random.normal(off_key, (2, width, width), jnp.float32), -4.0, 4.0)
    symmetric = 0.5 * (raw + jnp.swapaxes(raw, 1, 2))
    ident = (jnp.arange(width)[:, None] == jnp.arange(width)[None, :]).astype(jnp.float32)
    result = 0.8 * symmetric * (1.0 / math.sqrt(width)) * (1.0 - ident) + ident[None, :, :] * diagonal[:, :, None]
    return result.astype(jnp.bfloat16)


def block_levels(own_key, shape, pieces, smallest, top_value):
    level = 1.0
    for dim, parts in pieces:
        steps = jax.random.uniform(jax.random.fold_in(jax.random.fold_in(own_key, 6), dim), (parts,), jnp.float32, smallest / len(pieces), top_value / len(pieces))
        level = level * jnp.repeat(jnp.exp(steps), shape[dim] // parts).reshape((-1,) + (1,) * (len(shape) - 1 - dim))
    return level


def centred(key, dims, deviation, most, cuts=(), kind=jnp.bfloat16):
    factor_of = block_levels(key, dims, cuts, -0.22, 0.18) if cuts else 1.0
    entries = jax.random.normal(key, dims, jnp.float32) * deviation * factor_of
    return jnp.minimum(jnp.maximum(entries, -most), most).astype(kind)


def setup_inputs(seed: int = 0, part: int = 0) -> dict:
    seeds = jax.random.split(jax.random.key(seed), 12)
    own_keys = jax.random.split(jax.random.fold_in(seeds[11], part), 12)
    activations = centred(own_keys[0], (TOKENS, D), 1.0, 6.0, ((0, 32),))
    gate_values = centred(own_keys[1], (TOKENS, FF), 1.0, 6.0, ((0, 8), (1, 4)))
    up_values = centred(own_keys[2], (TOKENS, FF), 1.0, 6.0, ((0, 8), (1, 4)))
    cotangent = centred(own_keys[3], (TOKENS, D), 1.0, 6.0, ((0, 32),))
    down_weight = centred(seeds[4], (FF, D), D ** -0.5, 0.09375, ((0, 4), (1, 8)))
    up_entry = centred(seeds[5], (RANK, D), D ** -0.5, 0.09375)
    up_exit = centred(seeds[6], (RANK, FF), FF ** -0.5, 0.046875, ((1, 4),))
    down_entry = centred(seeds[7], (RANK, FF), FF ** -0.5, 0.046875, ((1, 4),))
    down_exit = centred(seeds[8], (RANK, D), D ** -0.5, 0.09375)
    queries = centred(seeds[9], (NQ, 2, K2), (2 * LEN * RANK * RANK) ** -0.5, 0.0029296875, ((0, 8), (2, 4)))
    fisher = draw_fisher(jax.random.fold_in(seeds[11], 71), part)
    return dict(activations=activations, gate_values=gate_values, up_values=up_values, cotangent=cotangent, down_weight=down_weight, up_entry=up_entry, up_exit=up_exit, down_entry=down_entry, down_exit=down_exit, queries=queries, fisher=fisher)


def reference(activations, gate_values, up_values, cotangent, down_weight, up_entry, up_exit, down_entry, down_exit, queries, fisher):
    highest = lax.Precision.HIGHEST

    def one_sequence(block):
        inputs, gates, ups, grads = block
        gate_f = gates.astype(jnp.float32)
        soft = jax.nn.silu(gate_f)
        act_down = (soft * ups.astype(jnp.float32)).astype(jnp.bfloat16)
        back_hidden = jnp.dot(grads, down_weight.T, preferred_element_type=jnp.float32)
        grad_up = (back_hidden * soft).astype(jnp.bfloat16)
        in_up = jnp.dot(inputs, up_entry.T, preferred_element_type=jnp.float32)
        out_up = jnp.dot(grad_up, up_exit.T, preferred_element_type=jnp.float32)
        in_down = jnp.dot(act_down, down_entry.T, preferred_element_type=jnp.float32)
        out_down = jnp.dot(grads, down_exit.T, preferred_element_type=jnp.float32)
        grad_first = jnp.dot(in_up.T, out_up, precision=highest).reshape(-1)
        grad_second = jnp.dot(in_down.T, out_down, precision=highest).reshape(-1)
        return jnp.stack([grad_first, grad_second])

    seq_grads = lax.map(one_sequence, (activations.reshape(SEQS, LEN, D), gate_values.reshape(SEQS, LEN, FF), up_values.reshape(SEQS, LEN, FF), cotangent.reshape(SEQS, LEN, D)))
    applied = jnp.einsum("lkj,slj->slk", fisher.astype(jnp.float32), seq_grads, precision=highest)
    flat_queries = queries.astype(jnp.float32).reshape(NQ, 2 * K2)
    return jnp.dot(flat_queries, applied.reshape(SEQS, 2 * K2).T, precision=highest)
```

```python
import functools

import jax
import jax.numpy as jnp
from jax import lax
from jax.experimental import pallas as pl
from jax.experimental.pallas import tpu as pltpu
from jax.sharding import PartitionSpec as P

LEN = 512
PAIR = 2
MESH = pl.DeviceIdType.MESH
HIGHEST = lax.Precision.HIGHEST
NT = (((1,), (1,)), ((), ()))
TN = (((0,), (0,)), ((), ()))
F32 = jnp.float32
BF16 = jnp.bfloat16


def silu(v):
    return v / (1.0 + jnp.exp(-v))


def halves(v):
    high = v.astype(BF16)
    low = (v - high.astype(F32)).astype(BF16)
    return jnp.concatenate([high, low], axis=0)


def kernel(
    dims,
    act_hbm,
    gate_hbm,
    up_hbm,
    cot_hbm,
    w_hbm,
    up_entry,
    up_exit,
    down_entry,
    down_exit,
    q_hbm,
    fisher_hbm,
    out_ref,
    wbuf,
    gbuf,
    ubuf,
    cotbuf,
    cloc,
    aloc,
    fbuf,
    qbuf,
    pbuf,
    out_acc,
    in_acc,
    gpart,
    abuf,
    gs,
    apart,
    bbuf,
    cpart,
    cbuf,
    ws_sem,
    wr_sem,
    gs_sem,
    gr_sem,
    loc_sem,
    snd_sem,
    rcv_sem,
):
    DP, FS, Z, T, TR, H, DL, CH, NC, R, S, SL, NI, KS, QS = dims
    N = DP * FS
    LAY = PAIR * FS
    gi = lax.axis_index("groups")
    d = lax.axis_index("dp")
    f = lax.axis_index("fsdp")
    z = lax.div(d, PAIR)
    y = lax.rem(d, PAIR)
    me = d * FS + f
    lm = y * FS + f

    def dev(flat):
        return (gi, lax.div(flat, FS), lax.rem(flat, FS))

    def lay_dev(q):
        return (gi, z * PAIR + lax.div(q, FS), lax.rem(q, FS))

    def remote(src, dst, ssem, rsem, to):
        return pltpu.make_async_remote_copy(
            src_ref=src, dst_ref=dst, send_sem=ssem, recv_sem=rsem, device_id=to, device_id_type=MESH
        )

    my_tok = pl.ds(pl.multiple_of(y * T, T), T)
    my_rows = pl.ds(pl.multiple_of(lm * TR, TR), TR)
    loads = [
        pltpu.make_async_copy(act_hbm, aloc, loc_sem.at[0]),
        pltpu.make_async_copy(cot_hbm, cloc, loc_sem.at[1]),
        pltpu.make_async_copy(gate_hbm, gbuf.at[my_tok, :], loc_sem.at[2]),
        pltpu.make_async_copy(up_hbm, ubuf, loc_sem.at[3]),
        pltpu.make_async_copy(w_hbm, wbuf.at[:, pl.ds(pl.multiple_of(z * DL, DL), DL)], loc_sem.at[4]),
        pltpu.make_async_copy(fisher_hbm, fbuf, loc_sem.at[5]),
    ]
    for load in loads:
        load.start()

    barrier = pltpu.get_barrier_semaphore()

    def greet(k, _):
        pl.semaphore_signal(barrier, inc=1, device_id=dev(lax.rem(me + k, N)), device_id_type=MESH)
        return 0

    lax.fori_loop(1, N, greet, 0)
    pl.semaphore_wait(barrier, N - 1)

    def wcopy(own, zz, c, way):
        rows = pl.ds(pl.multiple_of(c * CH, CH), CH)
        cols = pl.ds(pl.multiple_of(zz * DL, DL), DL)
        to = (z + 1 if way else z - 1) * PAIR + y
        src = w_hbm.at[rows, :] if own else wbuf.at[rows, cols]
        return remote(src, wbuf.at[rows, cols], ws_sem.at[way, zz, c], wr_sem.at[zz, c], (gi, to, f))

    def gcopy(c):
        cols = pl.ds(pl.multiple_of(c * CH, CH), CH)
        return remote(
            gate_hbm.at[:, cols],
            gbuf.at[my_tok, cols],
            gs_sem.at[c],
            gr_sem.at[c],
            (gi, z * PAIR + (1 - y), f),
        )

    def own_sends(c, _):
        @pl.when(z > 0)
        def _():
            wcopy(True, z, c, 0).start()

        @pl.when(z < Z - 1)
        def _():
            wcopy(True, z, c, 1).start()

        return 0

    lax.fori_loop(0, NC, own_sends, 0)

    def cot_piece(py, zz):
        return cot_hbm.at[:, pl.ds(pl.multiple_of((zz * PAIR + py) * DL, DL), DL)]

    for zz in range(Z):
        pltpu.make_async_copy(cot_piece(y, zz), cotbuf.at[my_rows, pl.ds(zz * DL, DL)], rcv_sem.at[0]).start()

    def cot_sends(k, _):
        q = lax.rem(lm + k, LAY)
        for zz in range(Z):
            remote(
                cot_piece(lax.div(q, FS), zz),
                cotbuf.at[my_rows, pl.ds(zz * DL, DL)],
                snd_sem.at[0],
                rcv_sem.at[0],
                lay_dev(q),
            ).start()
        return 0

    lax.fori_loop(1, LAY, cot_sends, 0)

    def gate_sends(c, _):
        gcopy(c).start()
        return 0

    lax.fori_loop(0, NC, gate_sends, 0)

    pltpu.make_async_copy(q_hbm.at[d], qbuf.at[d], rcv_sem.at[2]).start()

    def q_sends(k, _):
        to = lax.rem(d + k, DP)
        remote(q_hbm.at[to], qbuf.at[d], snd_sem.at[2], rcv_sem.at[2], (gi, to, f)).start()
        return 0

    lax.fori_loop(1, DP, q_sends, 0)

    loads[0].wait()
    loads[1].wait()
    pbuf[my_rows, 0:R] = lax.dot_general(aloc[...], up_entry[...], NT, preferred_element_type=F32)
    pbuf[my_rows, R : 2 * R] = lax.dot_general(cloc[...], down_exit[...], NT, preferred_element_type=F32)

    def p_sends(k, _):
        remote(
            pbuf.at[my_rows, :], pbuf.at[my_rows, :], snd_sem.at[1], rcv_sem.at[1], lay_dev(lax.rem(lm + k, LAY))
        ).start()
        return 0

    lax.fori_loop(1, LAY, p_sends, 0)

    TT = 256
    loads[2].wait()
    loads[3].wait()
    in_acc[...] = jnp.zeros_like(in_acc)
    out_acc[...] = jnp.zeros_like(out_acc)

    def down_chunk(c, _):
        cols = pl.ds(pl.multiple_of(c * CH, CH), CH)

        def down_tile(t, _):
            rows = pl.ds(pl.multiple_of(t * TT, TT), TT)
            grow = pl.ds(pl.multiple_of(y * T + t * TT, TT), TT)
            soft = silu(gbuf[grow, cols].astype(F32))
            hidden = (soft * ubuf[rows, cols].astype(F32)).astype(BF16)
            in_acc[rows, :] += lax.dot_general(hidden, down_entry[:, cols], NT, preferred_element_type=F32)
            return 0

        lax.fori_loop(0, T // TT, down_tile, 0)
        return 0

    lax.fori_loop(0, NC, down_chunk, 0)

    p_rest = pbuf.at[pl.ds(0, (LAY - 1) * TR), :]
    pltpu.make_async_copy(p_rest, p_rest, rcv_sem.at[1]).wait()
    for s in range(SL):
        rows = pl.ds(pl.multiple_of(y * T + s * LEN, LEN), LEN)
        g = lax.dot_general(
            in_acc[s * LEN : (s + 1) * LEN, :],
            pbuf[rows, R : 2 * R],
            TN,
            precision=HIGHEST,
            preferred_element_type=F32,
        )
        for dd in range(DP):
            gpart[dd, PAIR * SL + s] = g[dd * NI : (dd + 1) * NI, :]

    pltpu.make_async_copy(cotbuf, cotbuf, rcv_sem.at[0]).wait()
    loads[4].wait()

    def main_chunk(c, _):
        for k in range(1, Z):
            above = z + k
            below = z - k

            @pl.when(above < Z)
            def _():
                wcopy(False, above, c, 0).wait_recv()

            @pl.when((above < Z) & (z > 0))
            def _():
                wcopy(False, above, c, 0).start()

            @pl.when(below >= 0)
            def _():
                wcopy(False, below, c, 1).wait_recv()

            @pl.when((below >= 0) & (z < Z - 1))
            def _():
                wcopy(False, below, c, 1).start()

        cols = pl.ds(pl.multiple_of(c * CH, CH), CH)
        other = pl.ds(pl.multiple_of((1 - y) * T, T), T)
        remote(
            gate_hbm.at[:, cols], gbuf.at[other, cols], gs_sem.at[c], gr_sem.at[c], (gi, z * PAIR + (1 - y), f)
        ).wait_recv()

        def tile(t, _):
            rows = pl.ds(pl.multiple_of(t * TT, TT), TT)
            back = lax.dot_general(cotbuf[rows, :], wbuf[cols, :], NT, preferred_element_type=F32)
            grad = (back * silu(gbuf[rows, cols].astype(F32))).astype(BF16)
            out_acc[rows, :] += lax.dot_general(grad, up_exit[:, cols], NT, preferred_element_type=F32)
            return 0

        lax.fori_loop(0, PAIR * T // TT, tile, 0)
        return 0

    lax.fori_loop(0, NC, main_chunk, 0)

    for s in range(PAIR * SL):
        rows = slice(s * LEN, (s + 1) * LEN)
        g = lax.dot_general(pbuf[rows, 0:R], out_acc[rows, :], TN, precision=HIGHEST, preferred_element_type=F32)
        for dd in range(DP):
            gpart[dd, s] = g[dd * NI : (dd + 1) * NI, :]

    pltpu.make_async_copy(gpart.at[d], abuf.at[me], rcv_sem.at[3]).start()

    def a_sends(k, _):
        to = lax.rem(me + k, N)
        remote(gpart.at[lax.div(to, FS)], abuf.at[me], snd_sem.at[3], rcv_sem.at[3], dev(to)).start()
        return 0

    lax.fori_loop(1, N, a_sends, 0)
    loads[5].wait()
    pltpu.make_async_copy(abuf, abuf, rcv_sem.at[3]).wait()
    for zz in range(Z):
        total = abuf[zz * LAY, 0 : PAIR * SL]
        for m in range(1, LAY):
            total = total + abuf[zz * LAY + m, 0 : PAIR * SL]
        gs[0, zz * PAIR * SL : (zz + 1) * PAIR * SL] = total
    for dd in range(DP):
        total = abuf[dd * FS, PAIR * SL :]
        for m in range(1, FS):
            total = total + abuf[dd * FS + m, PAIR * SL :]
        gs[1, dd * SL : (dd + 1) * SL] = total
    for l in range(2):
        flat = jnp.concatenate([gs[l, :, i, :] for i in range(NI)], axis=1)
        both = lax.dot_general(halves(flat), fbuf[l], NT, preferred_element_type=F32)
        part = both[:S] + both[S:]
        for dd in range(DP):
            apart[dd, l * S : (l + 1) * S, :] = part[:, dd * KS : (dd + 1) * KS]

    pltpu.make_async_copy(apart.at[d], bbuf.at[d], rcv_sem.at[4]).start()

    def b_sends(k, _):
        to = lax.rem(d + k, DP)
        remote(apart.at[to], bbuf.at[d], snd_sem.at[4], rcv_sem.at[4], (gi, to, f)).start()
        return 0

    lax.fori_loop(1, DP, b_sends, 0)
    pltpu.make_async_copy(qbuf, qbuf, rcv_sem.at[2]).wait()
    pltpu.make_async_copy(bbuf, bbuf, rcv_sem.at[4]).wait()
    applied = bbuf[0]
    for dd in range(1, DP):
        applied = applied + bbuf[dd]
    wide = halves(jnp.concatenate([applied[:S], applied[S:]], axis=1))
    per = qbuf.shape[1]
    for dd in range(DP):
        both = lax.dot_general(wide, qbuf[dd], NT, preferred_element_type=F32)
        part = both[:S] + both[S:]
        for ff in range(FS):
            cpart[dd * FS + ff] = part[:, ff * QS : (ff + 1) * QS]

    pltpu.make_async_copy(cpart.at[me], cbuf.at[me], rcv_sem.at[5]).start()

    def c_sends(k, _):
        to = lax.rem(me + k, N)
        remote(cpart.at[to], cbuf.at[me], snd_sem.at[5], rcv_sem.at[5], dev(to)).start()
        return 0

    lax.fori_loop(1, N, c_sends, 0)

    def drain(ref, sem):
        pltpu.make_async_copy(ref, ref, sem).wait()

    for zz in range(Z):

        def chunk(c, _, zz=zz):
            @pl.when((z > 0) & (zz >= z))
            def _():
                wcopy(False, zz, c, 0).wait_send()

            @pl.when((z < Z - 1) & (zz <= z))
            def _():
                wcopy(False, zz, c, 1).wait_send()

            return 0

        lax.fori_loop(0, NC, chunk, 0)

    def gdrain(c, _):
        gcopy(c).wait_send()
        return 0

    lax.fori_loop(0, NC, gdrain, 0)
    drain(cotbuf.at[pl.ds(0, (LAY - 1) * TR), :], snd_sem.at[0])
    drain(p_rest, snd_sem.at[1])
    drain(qbuf.at[pl.ds(0, DP - 1)], snd_sem.at[2])
    drain(abuf.at[pl.ds(0, N - 1)], snd_sem.at[3])
    drain(bbuf.at[pl.ds(0, DP - 1)], snd_sem.at[4])
    drain(cbuf.at[pl.ds(0, N - 1)], snd_sem.at[5])

    drain(cbuf, rcv_sem.at[5])
    out_ref[...] = jnp.sum(cbuf[...], axis=0)


def local(
    shape,
    activations,
    gate_values,
    up_values,
    cotangent,
    down_weight,
    up_entry,
    up_exit,
    down_entry,
    down_exit,
    queries,
    fisher,
):
    DP, FS = shape
    Z = DP // PAIR
    T, H = gate_values.shape
    TR, D = cotangent.shape
    DL = down_weight.shape[1]
    R = up_entry.shape[0]
    CH = 256
    NC = H // CH
    SL = T // LEN
    S = DP * SL
    NI = fisher.shape[2] // R
    nq, _, kl = queries.shape
    KS = kl // DP
    N = DP * FS
    QS = nq // FS
    dims = (DP, FS, Z, T, TR, H, DL, CH, NC, R, S, SL, NI, KS, QS)
    moved = queries.reshape(nq, 2, DP, KS).transpose(2, 0, 1, 3).reshape(DP, nq, 2 * KS)
    hbm = pl.BlockSpec(memory_space=pl.ANY)
    vmem = pl.BlockSpec(memory_space=pltpu.VMEM)
    dma = pltpu.SemaphoreType.DMA
    out = pl.pallas_call(
        functools.partial(kernel, dims),
        out_shape=jax.ShapeDtypeStruct((S, QS), F32),
        in_specs=[hbm] * 5 + [vmem] * 4 + [hbm] * 2,
        out_specs=vmem,
        scratch_shapes=[
            pltpu.VMEM((H, Z * DL), BF16),
            pltpu.VMEM((PAIR * T, H), BF16),
            pltpu.VMEM((T, H), BF16),
            pltpu.VMEM((PAIR * T, Z * DL), BF16),
            pltpu.VMEM((TR, D), BF16),
            pltpu.VMEM((TR, D), BF16),
            pltpu.VMEM(fisher.shape, BF16),
            pltpu.VMEM((DP, nq, 2 * KS), BF16),
            pltpu.VMEM((PAIR * T, 2 * R), F32),
            pltpu.VMEM((PAIR * T, R), F32),
            pltpu.VMEM((T, R), F32),
            pltpu.VMEM((DP, (PAIR + 1) * SL, NI, R), F32),
            pltpu.VMEM((N, (PAIR + 1) * SL, NI, R), F32),
            pltpu.VMEM((2, S, NI, R), F32),
            pltpu.VMEM((DP, 2 * S, KS), F32),
            pltpu.VMEM((DP, 2 * S, KS), F32),
            pltpu.VMEM((N, S, QS), F32),
            pltpu.VMEM((N, S, QS), F32),
            dma((2, Z, NC)),
            dma((Z, NC)),
            dma((NC,)),
            dma((NC,)),
            dma((6,)),
            dma((6,)),
            dma((6,)),
        ],
        compiler_params=pltpu.CompilerParams(
            collective_id=0, has_side_effects=True, vmem_limit_bytes=58 * 1024 * 1024
        ),
    )(
        activations,
        gate_values,
        up_values,
        cotangent,
        down_weight,
        up_entry,
        up_exit,
        down_entry,
        down_exit,
        moved,
        fisher,
    )
    return out.T


def solution(mesh):
    placed = (
        P(("groups", "dp", "fsdp"), None),
        P(("groups", "dp"), "fsdp"),
        P(("groups", "dp"), "fsdp"),
        P(("groups", "dp", "fsdp"), None),
        P("fsdp", "dp"),
        P(),
        P(None, "fsdp"),
        P(None, "fsdp"),
        P(),
        P("dp", None, "fsdp"),
        P(None, "fsdp", "dp"),
    )
    return jax.shard_map(
        functools.partial(local, (mesh.shape["dp"], mesh.shape["fsdp"])),
        mesh=mesh,
        in_specs=placed,
        out_specs=P(("dp", "fsdp"), "groups"),
        check_vma=False,
    )
```

```python
import functools

import jax
import jax.numpy as jnp
from jax import lax
from jax.experimental import pallas as pl
from jax.experimental.pallas import tpu as pltpu
from jax.sharding import PartitionSpec as P

LEN = 512
PAIR = 2
MESH = pl.DeviceIdType.MESH
HIGHEST = lax.Precision.HIGHEST
NT = (((1,), (1,)), ((), ()))
TN = (((0,), (0,)), ((), ()))
F32 = jnp.float32
BF16 = jnp.bfloat16


def silu(v):
    return v / (1.0 + jnp.exp(-v))


def halves(v):
    high = v.astype(BF16)
    low = (v - high.astype(F32)).astype(BF16)
    return jnp.concatenate([high, low], axis=0)


def kernel(
    dims,
    act_hbm,
    gate_hbm,
    up_hbm,
    cot_hbm,
    w_hbm,
    up_entry,
    up_exit,
    down_entry,
    down_exit,
    q_hbm,
    fisher_hbm,
    out_ref,
    wbuf,
    gbuf,
    ubuf,
    cotbuf,
    cloc,
    aloc,
    fbuf,
    qbuf,
    pbuf,
    out_acc,
    in_acc,
    gpart,
    abuf,
    gs,
    apart,
    bbuf,
    cpart,
    cbuf,
    ws_sem,
    wr_sem,
    gs_sem,
    gr_sem,
    loc_sem,
    snd_sem,
    rcv_sem,
):
    DP, FS, Z, T, TR, H, DL, CH, NC, R, S, SL, NI, KS, QS = dims
    N = DP * FS
    LAY = PAIR * FS
    gi = lax.axis_index("groups")
    d = lax.axis_index("dp")
    f = lax.axis_index("fsdp")
    z = lax.div(d, PAIR)
    y = lax.rem(d, PAIR)
    me = d * FS + f
    lm = y * FS + f

    def dev(flat):
        return (gi, lax.div(flat, FS), lax.rem(flat, FS))

    def lay_dev(q):
        return (gi, z * PAIR + lax.div(q, FS), lax.rem(q, FS))

    def remote(src, dst, ssem, rsem, to):
        return pltpu.make_async_remote_copy(
            src_ref=src, dst_ref=dst, send_sem=ssem, recv_sem=rsem, device_id=to, device_id_type=MESH
        )

    my_tok = pl.ds(pl.multiple_of(y * T, T), T)
    my_rows = pl.ds(pl.multiple_of(lm * TR, TR), TR)
    loads = [
        pltpu.make_async_copy(act_hbm, aloc, loc_sem.at[0]),
        pltpu.make_async_copy(cot_hbm, cloc, loc_sem.at[1]),
        pltpu.make_async_copy(gate_hbm, gbuf.at[my_tok, :], loc_sem.at[2]),
        pltpu.make_async_copy(up_hbm, ubuf, loc_sem.at[3]),
        pltpu.make_async_copy(w_hbm, wbuf.at[:, pl.ds(pl.multiple_of(z * DL, DL), DL)], loc_sem.at[4]),
        pltpu.make_async_copy(fisher_hbm, fbuf, loc_sem.at[5]),
    ]
    for load in loads:
        load.start()

    barrier = pltpu.get_barrier_semaphore()

    def greet(k, _):
        pl.semaphore_signal(barrier, inc=1, device_id=dev(lax.rem(me + k, N)), device_id_type=MESH)
        return 0

    lax.fori_loop(1, N, greet, 0)
    pl.semaphore_wait(barrier, N - 1)

    def wcopy(own, zz, c, way):
        rows = pl.ds(pl.multiple_of(c * CH, CH), CH)
        cols = pl.ds(pl.multiple_of(zz * DL, DL), DL)
        to = (z + 1 if way else z - 1) * PAIR + y
        src = w_hbm.at[rows, :] if own else wbuf.at[rows, cols]
        return remote(src, wbuf.at[rows, cols], ws_sem.at[way, zz, c], wr_sem.at[zz, c], (gi, to, f))

    def gcopy(c):
        cols = pl.ds(pl.multiple_of(c * CH, CH), CH)
        return remote(
            gate_hbm.at[:, cols],
            gbuf.at[my_tok, cols],
            gs_sem.at[c],
            gr_sem.at[c],
            (gi, z * PAIR + (1 - y), f),
        )

    def own_sends(c, _):
        @pl.when(z > 0)
        def _():
            wcopy(True, z, c, 0).start()

        @pl.when(z < Z - 1)
        def _():
            wcopy(True, z, c, 1).start()

        return 0


    def cot_piece(py, zz):
        return cot_hbm.at[:, pl.ds(pl.multiple_of((zz * PAIR + py) * DL, DL), DL)]

    for zz in range(Z):
        pltpu.make_async_copy(cot_piece(y, zz), cotbuf.at[my_rows, pl.ds(zz * DL, DL)], rcv_sem.at[0]).start()

    def cot_sends(k, _):
        q = lax.rem(lm + k, LAY)
        for zz in range(Z):
            remote(
                cot_piece(lax.div(q, FS), zz),
                cotbuf.at[my_rows, pl.ds(zz * DL, DL)],
                snd_sem.at[0],
                rcv_sem.at[0],
                lay_dev(q),
            ).start()
        return 0

    lax.fori_loop(1, LAY, cot_sends, 0)

    lax.fori_loop(0, NC, own_sends, 0)

    pltpu.make_async_copy(q_hbm.at[d], qbuf.at[d], rcv_sem.at[2]).start()

    def q_sends(k, _):
        to = lax.rem(d + k, DP)
        remote(q_hbm.at[to], qbuf.at[d], snd_sem.at[2], rcv_sem.at[2], (gi, to, f)).start()
        return 0

    lax.fori_loop(1, DP, q_sends, 0)

    loads[0].wait()
    loads[1].wait()
    pbuf[my_rows, 0:R] = lax.dot_general(aloc[...], up_entry[...], NT, preferred_element_type=F32)
    pbuf[my_rows, R : 2 * R] = lax.dot_general(cloc[...], down_exit[...], NT, preferred_element_type=F32)

    def p_sends(k, _):
        remote(
            pbuf.at[my_rows, :], pbuf.at[my_rows, :], snd_sem.at[1], rcv_sem.at[1], lay_dev(lax.rem(lm + k, LAY))
        ).start()
        return 0

    lax.fori_loop(1, LAY, p_sends, 0)

    TT = 256
    loads[2].wait()
    loads[3].wait()
    in_acc[...] = jnp.zeros_like(in_acc)
    out_acc[...] = jnp.zeros_like(out_acc)

    def down_chunk(c, _):
        cols = pl.ds(pl.multiple_of(c * CH, CH), CH)

        def down_tile(t, _):
            rows = pl.ds(pl.multiple_of(t * TT, TT), TT)
            grow = pl.ds(pl.multiple_of(y * T + t * TT, TT), TT)
            soft = silu(gbuf[grow, cols].astype(F32))
            hidden = (soft * ubuf[rows, cols].astype(F32)).astype(BF16)
            in_acc[rows, :] += lax.dot_general(hidden, down_entry[:, cols], NT, preferred_element_type=F32)
            return 0

        lax.fori_loop(0, T // TT, down_tile, 0)
        return 0

    lax.fori_loop(0, NC, down_chunk, 0)

    p_rest = pbuf.at[pl.ds(0, (LAY - 1) * TR), :]
    pltpu.make_async_copy(p_rest, p_rest, rcv_sem.at[1]).wait()
    for s in range(SL):
        rows = pl.ds(pl.multiple_of(y * T + s * LEN, LEN), LEN)
        g = lax.dot_general(
            in_acc[s * LEN : (s + 1) * LEN, :],
            pbuf[rows, R : 2 * R],
            TN,
            precision=HIGHEST,
            preferred_element_type=F32,
        )
        for dd in range(DP):
            gpart[dd, PAIR * SL + s] = g[dd * NI : (dd + 1) * NI, :]

    pltpu.make_async_copy(cotbuf, cotbuf, rcv_sem.at[0]).wait()
    loads[4].wait()

    gcopy(0).start()
    gcopy(1).start()
    gcopy(2).start()

    def main_chunk(c, _):
        for k in range(1, Z):
            above = z + k
            below = z - k

            @pl.when(above < Z)
            def _():
                wcopy(False, above, c, 0).wait_recv()

            @pl.when((above < Z) & (z > 0))
            def _():
                wcopy(False, above, c, 0).start()

            @pl.when(below >= 0)
            def _():
                wcopy(False, below, c, 1).wait_recv()

            @pl.when((below >= 0) & (z < Z - 1))
            def _():
                wcopy(False, below, c, 1).start()

        cols = pl.ds(pl.multiple_of(c * CH, CH), CH)
        @pl.when(c + 3 < NC)
        def _():
            gcopy(c + 3).start()

        other = pl.ds(pl.multiple_of((1 - y) * T, T), T)
        remote(
            gate_hbm.at[:, cols], gbuf.at[other, cols], gs_sem.at[c], gr_sem.at[c], (gi, z * PAIR + (1 - y), f)
        ).wait_recv()

        def tile(t, _):
            rows = pl.ds(pl.multiple_of(t * TT, TT), TT)
            back = lax.dot_general(cotbuf[rows, :], wbuf[cols, :], NT, preferred_element_type=F32)
            grad = (back * silu(gbuf[rows, cols].astype(F32))).astype(BF16)
            out_acc[rows, :] += lax.dot_general(grad, up_exit[:, cols], NT, preferred_element_type=F32)
            return 0

        lax.fori_loop(0, PAIR * T // TT, tile, 0)
        return 0

    lax.fori_loop(0, NC, main_chunk, 0)

    for s in range(PAIR * SL):
        rows = slice(s * LEN, (s + 1) * LEN)
        g = lax.dot_general(pbuf[rows, 0:R], out_acc[rows, :], TN, precision=HIGHEST, preferred_element_type=F32)
        for dd in range(DP):
            gpart[dd, s] = g[dd * NI : (dd + 1) * NI, :]

    pltpu.make_async_copy(gpart.at[d], abuf.at[me], rcv_sem.at[3]).start()

    def a_sends(k, _):
        to = lax.rem(me + k, N)
        remote(gpart.at[lax.div(to, FS)], abuf.at[me], snd_sem.at[3], rcv_sem.at[3], dev(to)).start()
        return 0

    lax.fori_loop(1, N, a_sends, 0)
    loads[5].wait()
    pltpu.make_async_copy(abuf, abuf, rcv_sem.at[3]).wait()
    for zz in range(Z):
        total = abuf[zz * LAY, 0 : PAIR * SL]
        for m in range(1, LAY):
            total = total + abuf[zz * LAY + m, 0 : PAIR * SL]
        gs[0, zz * PAIR * SL : (zz + 1) * PAIR * SL] = total
    for dd in range(DP):
        total = abuf[dd * FS, PAIR * SL :]
        for m in range(1, FS):
            total = total + abuf[dd * FS + m, PAIR * SL :]
        gs[1, dd * SL : (dd + 1) * SL] = total
    for l in range(2):
        flat = jnp.concatenate([gs[l, :, i, :] for i in range(NI)], axis=1)
        both = lax.dot_general(halves(flat), fbuf[l], NT, preferred_element_type=F32)
        part = both[:S] + both[S:]
        for dd in range(DP):
            apart[dd, l * S : (l + 1) * S, :] = part[:, dd * KS : (dd + 1) * KS]

    pltpu.make_async_copy(apart.at[d], bbuf.at[d], rcv_sem.at[4]).start()

    def b_sends(k, _):
        to = lax.rem(d + k, DP)
        remote(apart.at[to], bbuf.at[d], snd_sem.at[4], rcv_sem.at[4], (gi, to, f)).start()
        return 0

    lax.fori_loop(1, DP, b_sends, 0)
    pltpu.make_async_copy(qbuf, qbuf, rcv_sem.at[2]).wait()
    pltpu.make_async_copy(bbuf, bbuf, rcv_sem.at[4]).wait()
    applied = bbuf[0]
    for dd in range(1, DP):
        applied = applied + bbuf[dd]
    wide = halves(jnp.concatenate([applied[:S], applied[S:]], axis=1))
    per = qbuf.shape[1]
    for dd in range(DP):
        both = lax.dot_general(wide, qbuf[dd], NT, preferred_element_type=F32)
        part = both[:S] + both[S:]
        for ff in range(FS):
            cpart[dd * FS + ff] = part[:, ff * QS : (ff + 1) * QS]

    pltpu.make_async_copy(cpart.at[me], cbuf.at[me], rcv_sem.at[5]).start()

    def c_sends(k, _):
        to = lax.rem(me + k, N)
        remote(cpart.at[to], cbuf.at[me], snd_sem.at[5], rcv_sem.at[5], dev(to)).start()
        return 0

    lax.fori_loop(1, N, c_sends, 0)

    def drain(ref, sem):
        pltpu.make_async_copy(ref, ref, sem).wait()

    for zz in range(Z):

        def chunk(c, _, zz=zz):
            @pl.when((z > 0) & (zz >= z))
            def _():
                wcopy(False, zz, c, 0).wait_send()

            @pl.when((z < Z - 1) & (zz <= z))
            def _():
                wcopy(False, zz, c, 1).wait_send()

            return 0

        lax.fori_loop(0, NC, chunk, 0)

    def gdrain(c, _):
        gcopy(c).wait_send()
        return 0

    lax.fori_loop(0, NC, gdrain, 0)
    drain(cotbuf.at[pl.ds(0, (LAY - 1) * TR), :], snd_sem.at[0])
    drain(p_rest, snd_sem.at[1])
    drain(qbuf.at[pl.ds(0, DP - 1)], snd_sem.at[2])
    drain(abuf.at[pl.ds(0, N - 1)], snd_sem.at[3])
    drain(bbuf.at[pl.ds(0, DP - 1)], snd_sem.at[4])
    drain(cbuf.at[pl.ds(0, N - 1)], snd_sem.at[5])

    drain(cbuf, rcv_sem.at[5])
    out_ref[...] = jnp.sum(cbuf[...], axis=0)


def local(
    shape,
    activations,
    gate_values,
    up_values,
    cotangent,
    down_weight,
    up_entry,
    up_exit,
    down_entry,
    down_exit,
    queries,
    fisher,
):
    DP, FS = shape
    Z = DP // PAIR
    T, H = gate_values.shape
    TR, D = cotangent.shape
    DL = down_weight.shape[1]
    R = up_entry.shape[0]
    CH = 256
    NC = H // CH
    SL = T // LEN
    S = DP * SL
    NI = fisher.shape[2] // R
    nq, _, kl = queries.shape
    KS = kl // DP
    N = DP * FS
    QS = nq // FS
    dims = (DP, FS, Z, T, TR, H, DL, CH, NC, R, S, SL, NI, KS, QS)
    moved = queries.reshape(nq, 2, DP, KS).transpose(2, 0, 1, 3).reshape(DP, nq, 2 * KS)
    hbm = pl.BlockSpec(memory_space=pl.ANY)
    vmem = pl.BlockSpec(memory_space=pltpu.VMEM)
    dma = pltpu.SemaphoreType.DMA
    out = pl.pallas_call(
        functools.partial(kernel, dims),
        out_shape=jax.ShapeDtypeStruct((S, QS), F32),
        in_specs=[hbm] * 5 + [vmem] * 4 + [hbm] * 2,
        out_specs=vmem,
        scratch_shapes=[
            pltpu.VMEM((H, Z * DL), BF16),
            pltpu.VMEM((PAIR * T, H), BF16),
            pltpu.VMEM((T, H), BF16),
            pltpu.VMEM((PAIR * T, Z * DL), BF16),
            pltpu.VMEM((TR, D), BF16),
            pltpu.VMEM((TR, D), BF16),
            pltpu.VMEM(fisher.shape, BF16),
            pltpu.VMEM((DP, nq, 2 * KS), BF16),
            pltpu.VMEM((PAIR * T, 2 * R), F32),
            pltpu.VMEM((PAIR * T, R), F32),
            pltpu.VMEM((T, R), F32),
            pltpu.VMEM((DP, (PAIR + 1) * SL, NI, R), F32),
            pltpu.VMEM((N, (PAIR + 1) * SL, NI, R), F32),
            pltpu.VMEM((2, S, NI, R), F32),
            pltpu.VMEM((DP, 2 * S, KS), F32),
            pltpu.VMEM((DP, 2 * S, KS), F32),
            pltpu.VMEM((N, S, QS), F32),
            pltpu.VMEM((N, S, QS), F32),
            dma((2, Z, NC)),
            dma((Z, NC)),
            dma((NC,)),
            dma((NC,)),
            dma((6,)),
            dma((6,)),
            dma((6,)),
        ],
        compiler_params=pltpu.CompilerParams(
            collective_id=0, has_side_effects=True, vmem_limit_bytes=58 * 1024 * 1024
        ),
    )(
        activations,
        gate_values,
        up_values,
        cotangent,
        down_weight,
        up_entry,
        up_exit,
        down_entry,
        down_exit,
        moved,
        fisher,
    )
    return out.T


def solution(mesh):
    placed = (
        P(("groups", "dp", "fsdp"), None),
        P(("groups", "dp"), "fsdp"),
        P(("groups", "dp"), "fsdp"),
        P(("groups", "dp", "fsdp"), None),
        P("fsdp", "dp"),
        P(),
        P(None, "fsdp"),
        P(None, "fsdp"),
        P(),
        P("dp", None, "fsdp"),
        P(None, "fsdp", "dp"),
    )
    return jax.shard_map(
        functools.partial(local, (mesh.shape["dp"], mesh.shape["fsdp"])),
        mesh=mesh,
        in_specs=placed,
        out_specs=P(("dp", "fsdp"), "groups"),
        check_vma=False,
    )
```

```python
import functools

import jax
import jax.numpy as jnp
from jax import lax
from jax.experimental import pallas as pl
from jax.experimental.pallas import tpu as pltpu
from jax.sharding import PartitionSpec as P

LEN = 512
PAIR = 2
MESH = pl.DeviceIdType.MESH
HIGHEST = lax.Precision.HIGHEST
NT = (((1,), (1,)), ((), ()))
TN = (((0,), (0,)), ((), ()))
F32 = jnp.float32
BF16 = jnp.bfloat16


def silu(v):
    return v / (1.0 + jnp.exp(-v))


def halves(v):
    high = v.astype(BF16)
    low = (v - high.astype(F32)).astype(BF16)
    return jnp.concatenate([high, low], axis=0)


def kernel(
    dims,
    act_hbm,
    gate_hbm,
    up_hbm,
    cot_hbm,
    w_hbm,
    up_entry,
    up_exit,
    down_entry,
    down_exit,
    q_hbm,
    fisher_hbm,
    out_ref,
    wbuf,
    gbuf,
    ubuf,
    cotbuf,
    cloc,
    aloc,
    fbuf,
    qbuf,
    pbuf,
    out_acc,
    in_acc,
    gpart,
    abuf,
    gs,
    apart,
    bbuf,
    cpart,
    cbuf,
    ws_sem,
    wr_sem,
    gs_sem,
    gr_sem,
    loc_sem,
    snd_sem,
    rcv_sem,
):
    DP, FS, Z, T, TR, H, DL, CH, NC, R, S, SL, NI, KS, QS = dims
    N = DP * FS
    LAY = PAIR * FS
    gi = lax.axis_index("groups")
    d = lax.axis_index("dp")
    f = lax.axis_index("fsdp")
    z = lax.div(d, PAIR)
    y = lax.rem(d, PAIR)
    me = d * FS + f
    lm = y * FS + f

    def dev(flat):
        return (gi, lax.div(flat, FS), lax.rem(flat, FS))

    def lay_dev(q):
        return (gi, z * PAIR + lax.div(q, FS), lax.rem(q, FS))

    def remote(src, dst, ssem, rsem, to):
        return pltpu.make_async_remote_copy(
            src_ref=src, dst_ref=dst, send_sem=ssem, recv_sem=rsem, device_id=to, device_id_type=MESH
        )

    my_tok = pl.ds(pl.multiple_of(y * T, T), T)
    my_rows = pl.ds(pl.multiple_of(lm * TR, TR), TR)
    loads = [
        pltpu.make_async_copy(act_hbm, aloc, loc_sem.at[0]),
        pltpu.make_async_copy(cot_hbm, cloc, loc_sem.at[1]),
        pltpu.make_async_copy(gate_hbm, gbuf.at[my_tok, :], loc_sem.at[2]),
        pltpu.make_async_copy(up_hbm, ubuf, loc_sem.at[3]),
        pltpu.make_async_copy(w_hbm, wbuf.at[:, pl.ds(pl.multiple_of(z * DL, DL), DL)], loc_sem.at[4]),
        pltpu.make_async_copy(fisher_hbm, fbuf, loc_sem.at[5]),
    ]
    for load in loads:
        load.start()

    barrier = pltpu.get_barrier_semaphore()

    def greet(k, _):
        pl.semaphore_signal(barrier, inc=1, device_id=dev(lax.rem(me + k, N)), device_id_type=MESH)
        return 0

    lax.fori_loop(1, N, greet, 0)
    pl.semaphore_wait(barrier, N - 1)

    def wcopy(own, zz, c, way):
        rows = pl.ds(pl.multiple_of(c * CH, CH), CH)
        cols = pl.ds(pl.multiple_of(zz * DL, DL), DL)
        to = (z + 1 if way else z - 1) * PAIR + y
        src = w_hbm.at[rows, :] if own else wbuf.at[rows, cols]
        return remote(src, wbuf.at[rows, cols], ws_sem.at[way, zz, c], wr_sem.at[zz, c], (gi, to, f))

    def gcopy(c):
        cols = pl.ds(pl.multiple_of(c * CH, CH), CH)
        return remote(
            gate_hbm.at[:, cols],
            gbuf.at[my_tok, cols],
            gs_sem.at[c],
            gr_sem.at[c],
            (gi, z * PAIR + (1 - y), f),
        )

    def own_sends(c, _):
        @pl.when(z > 0)
        def _():
            wcopy(True, z, c, 0).start()

        @pl.when(z < Z - 1)
        def _():
            wcopy(True, z, c, 1).start()

        return 0


    FIRST = min(4, NC)
    lax.fori_loop(0, FIRST, own_sends, 0)

    def cot_piece(py, zz):
        return cot_hbm.at[:, pl.ds(pl.multiple_of((zz * PAIR + py) * DL, DL), DL)]

    for zz in range(Z):
        pltpu.make_async_copy(cot_piece(y, zz), cotbuf.at[my_rows, pl.ds(zz * DL, DL)], rcv_sem.at[0]).start()

    def cot_sends(k, _):
        q = lax.rem(lm + k, LAY)
        for zz in range(Z):
            remote(
                cot_piece(lax.div(q, FS), zz),
                cotbuf.at[my_rows, pl.ds(zz * DL, DL)],
                snd_sem.at[0],
                rcv_sem.at[0],
                lay_dev(q),
            ).start()
        return 0

    lax.fori_loop(1, LAY, cot_sends, 0)

    lax.fori_loop(FIRST, NC, own_sends, 0)

    pltpu.make_async_copy(q_hbm.at[d], qbuf.at[d], rcv_sem.at[2]).start()

    def q_sends(k, _):
        to = lax.rem(d + k, DP)
        remote(q_hbm.at[to], qbuf.at[d], snd_sem.at[2], rcv_sem.at[2], (gi, to, f)).start()
        return 0

    lax.fori_loop(1, DP, q_sends, 0)

    loads[0].wait()
    loads[1].wait()
    pbuf[my_rows, 0:R] = lax.dot_general(aloc[...], up_entry[...], NT, preferred_element_type=F32)
    pbuf[my_rows, R : 2 * R] = lax.dot_general(cloc[...], down_exit[...], NT, preferred_element_type=F32)

    def p_sends(k, _):
        remote(
            pbuf.at[my_rows, :], pbuf.at[my_rows, :], snd_sem.at[1], rcv_sem.at[1], lay_dev(lax.rem(lm + k, LAY))
        ).start()
        return 0

    lax.fori_loop(1, LAY, p_sends, 0)

    TT = 256
    loads[2].wait()
    loads[3].wait()
    in_acc[...] = jnp.zeros_like(in_acc)
    out_acc[...] = jnp.zeros_like(out_acc)

    def down_chunk(c, _):
        cols = pl.ds(pl.multiple_of(c * CH, CH), CH)

        def down_tile(t, _):
            rows = pl.ds(pl.multiple_of(t * TT, TT), TT)
            grow = pl.ds(pl.multiple_of(y * T + t * TT, TT), TT)
            soft = silu(gbuf[grow, cols].astype(F32))
            hidden = (soft * ubuf[rows, cols].astype(F32)).astype(BF16)
            in_acc[rows, :] += lax.dot_general(hidden, down_entry[:, cols], NT, preferred_element_type=F32)
            return 0

        lax.fori_loop(0, T // TT, down_tile, 0)
        return 0

    lax.fori_loop(0, NC, down_chunk, 0)

    p_rest = pbuf.at[pl.ds(0, (LAY - 1) * TR), :]
    pltpu.make_async_copy(p_rest, p_rest, rcv_sem.at[1]).wait()
    for s in range(SL):
        rows = pl.ds(pl.multiple_of(y * T + s * LEN, LEN), LEN)
        g = lax.dot_general(
            in_acc[s * LEN : (s + 1) * LEN, :],
            pbuf[rows, R : 2 * R],
            TN,
            precision=HIGHEST,
            preferred_element_type=F32,
        )
        for dd in range(DP):
            gpart[dd, PAIR * SL + s] = g[dd * NI : (dd + 1) * NI, :]

    pltpu.make_async_copy(cotbuf, cotbuf, rcv_sem.at[0]).wait()
    loads[4].wait()

    gcopy(0).start()
    gcopy(1).start()
    gcopy(2).start()

    def main_chunk(c, _):
        for k in range(1, Z):
            above = z + k
            below = z - k

            @pl.when(above < Z)
            def _():
                wcopy(False, above, c, 0).wait_recv()

            @pl.when((above < Z) & (z > 0))
            def _():
                wcopy(False, above, c, 0).start()

            @pl.when(below >= 0)
            def _():
                wcopy(False, below, c, 1).wait_recv()

            @pl.when((below >= 0) & (z < Z - 1))
            def _():
                wcopy(False, below, c, 1).start()

        cols = pl.ds(pl.multiple_of(c * CH, CH), CH)
        @pl.when(c + 3 < NC)
        def _():
            gcopy(c + 3).start()

        other = pl.ds(pl.multiple_of((1 - y) * T, T), T)
        remote(
            gate_hbm.at[:, cols], gbuf.at[other, cols], gs_sem.at[c], gr_sem.at[c], (gi, z * PAIR + (1 - y), f)
        ).wait_recv()

        def tile(t, _):
            rows = pl.ds(pl.multiple_of(t * TT, TT), TT)
            back = lax.dot_general(cotbuf[rows, :], wbuf[cols, :], NT, preferred_element_type=F32)
            grad = (back * silu(gbuf[rows, cols].astype(F32))).astype(BF16)
            out_acc[rows, :] += lax.dot_general(grad, up_exit[:, cols], NT, preferred_element_type=F32)
            return 0

        lax.fori_loop(0, PAIR * T // TT, tile, 0)
        return 0

    lax.fori_loop(0, NC, main_chunk, 0)

    for s in range(PAIR * SL):
        rows = slice(s * LEN, (s + 1) * LEN)
        g = lax.dot_general(pbuf[rows, 0:R], out_acc[rows, :], TN, precision=HIGHEST, preferred_element_type=F32)
        for dd in range(DP):
            gpart[dd, s] = g[dd * NI : (dd + 1) * NI, :]

    pltpu.make_async_copy(gpart.at[d], abuf.at[me], rcv_sem.at[3]).start()

    def a_sends(k, _):
        to = lax.rem(me + k, N)
        remote(gpart.at[lax.div(to, FS)], abuf.at[me], snd_sem.at[3], rcv_sem.at[3], dev(to)).start()
        return 0

    lax.fori_loop(1, N, a_sends, 0)
    loads[5].wait()
    pltpu.make_async_copy(abuf, abuf, rcv_sem.at[3]).wait()
    for zz in range(Z):
        total = abuf[zz * LAY, 0 : PAIR * SL]
        for m in range(1, LAY):
            total = total + abuf[zz * LAY + m, 0 : PAIR * SL]
        gs[0, zz * PAIR * SL : (zz + 1) * PAIR * SL] = total
    for dd in range(DP):
        total = abuf[dd * FS, PAIR * SL :]
        for m in range(1, FS):
            total = total + abuf[dd * FS + m, PAIR * SL :]
        gs[1, dd * SL : (dd + 1) * SL] = total
    for l in range(2):
        flat = jnp.concatenate([gs[l, :, i, :] for i in range(NI)], axis=1)
        both = lax.dot_general(halves(flat), fbuf[l], NT, preferred_element_type=F32)
        part = both[:S] + both[S:]
        for dd in range(DP):
            apart[dd, l * S : (l + 1) * S, :] = part[:, dd * KS : (dd + 1) * KS]

    pltpu.make_async_copy(apart.at[d], bbuf.at[d], rcv_sem.at[4]).start()

    def b_sends(k, _):
        to = lax.rem(d + k, DP)
        remote(apart.at[to], bbuf.at[d], snd_sem.at[4], rcv_sem.at[4], (gi, to, f)).start()
        return 0

    lax.fori_loop(1, DP, b_sends, 0)
    pltpu.make_async_copy(qbuf, qbuf, rcv_sem.at[2]).wait()
    pltpu.make_async_copy(bbuf, bbuf, rcv_sem.at[4]).wait()
    applied = bbuf[0]
    for dd in range(1, DP):
        applied = applied + bbuf[dd]
    wide = halves(jnp.concatenate([applied[:S], applied[S:]], axis=1))
    per = qbuf.shape[1]
    for dd in range(DP):
        both = lax.dot_general(wide, qbuf[dd], NT, preferred_element_type=F32)
        part = both[:S] + both[S:]
        for ff in range(FS):
            cpart[dd * FS + ff] = part[:, ff * QS : (ff + 1) * QS]

    pltpu.make_async_copy(cpart.at[me], cbuf.at[me], rcv_sem.at[5]).start()

    def c_sends(k, _):
        to = lax.rem(me + k, N)
        remote(cpart.at[to], cbuf.at[me], snd_sem.at[5], rcv_sem.at[5], dev(to)).start()
        return 0

    lax.fori_loop(1, N, c_sends, 0)

    def drain(ref, sem):
        pltpu.make_async_copy(ref, ref, sem).wait()

    for zz in range(Z):

        def chunk(c, _, zz=zz):
            @pl.when((z > 0) & (zz >= z))
            def _():
                wcopy(False, zz, c, 0).wait_send()

            @pl.when((z < Z - 1) & (zz <= z))
            def _():
                wcopy(False, zz, c, 1).wait_send()

            return 0

        lax.fori_loop(0, NC, chunk, 0)

    def gdrain(c, _):
        gcopy(c).wait_send()
        return 0

    lax.fori_loop(0, NC, gdrain, 0)
    drain(cotbuf.at[pl.ds(0, (LAY - 1) * TR), :], snd_sem.at[0])
    drain(p_rest, snd_sem.at[1])
    drain(qbuf.at[pl.ds(0, DP - 1)], snd_sem.at[2])
    drain(abuf.at[pl.ds(0, N - 1)], snd_sem.at[3])
    drain(bbuf.at[pl.ds(0, DP - 1)], snd_sem.at[4])
    drain(cbuf.at[pl.ds(0, N - 1)], snd_sem.at[5])

    drain(cbuf, rcv_sem.at[5])
    out_ref[...] = jnp.sum(cbuf[...], axis=0)


def local(
    shape,
    activations,
    gate_values,
    up_values,
    cotangent,
    down_weight,
    up_entry,
    up_exit,
    down_entry,
    down_exit,
    queries,
    fisher,
):
    DP, FS = shape
    Z = DP // PAIR
    T, H = gate_values.shape
    TR, D = cotangent.shape
    DL = down_weight.shape[1]
    R = up_entry.shape[0]
    CH = 256
    NC = H // CH
    SL = T // LEN
    S = DP * SL
    NI = fisher.shape[2] // R
    nq, _, kl = queries.shape
    KS = kl // DP
    N = DP * FS
    QS = nq // FS
    dims = (DP, FS, Z, T, TR, H, DL, CH, NC, R, S, SL, NI, KS, QS)
    moved = queries.reshape(nq, 2, DP, KS).transpose(2, 0, 1, 3).reshape(DP, nq, 2 * KS)
    hbm = pl.BlockSpec(memory_space=pl.ANY)
    vmem = pl.BlockSpec(memory_space=pltpu.VMEM)
    dma = pltpu.SemaphoreType.DMA
    out = pl.pallas_call(
        functools.partial(kernel, dims),
        out_shape=jax.ShapeDtypeStruct((S, QS), F32),
        in_specs=[hbm] * 5 + [vmem] * 4 + [hbm] * 2,
        out_specs=vmem,
        scratch_shapes=[
            pltpu.VMEM((H, Z * DL), BF16),
            pltpu.VMEM((PAIR * T, H), BF16),
            pltpu.VMEM((T, H), BF16),
            pltpu.VMEM((PAIR * T, Z * DL), BF16),
            pltpu.VMEM((TR, D), BF16),
            pltpu.VMEM((TR, D), BF16),
            pltpu.VMEM(fisher.shape, BF16),
            pltpu.VMEM((DP, nq, 2 * KS), BF16),
            pltpu.VMEM((PAIR * T, 2 * R), F32),
            pltpu.VMEM((PAIR * T, R), F32),
            pltpu.VMEM((T, R), F32),
            pltpu.VMEM((DP, (PAIR + 1) * SL, NI, R), F32),
            pltpu.VMEM((N, (PAIR + 1) * SL, NI, R), F32),
            pltpu.VMEM((2, S, NI, R), F32),
            pltpu.VMEM((DP, 2 * S, KS), F32),
            pltpu.VMEM((DP, 2 * S, KS), F32),
            pltpu.VMEM((N, S, QS), F32),
            pltpu.VMEM((N, S, QS), F32),
            dma((2, Z, NC)),
            dma((Z, NC)),
            dma((NC,)),
            dma((NC,)),
            dma((6,)),
            dma((6,)),
            dma((6,)),
        ],
        compiler_params=pltpu.CompilerParams(
            collective_id=0, has_side_effects=True, vmem_limit_bytes=58 * 1024 * 1024
        ),
    )(
        activations,
        gate_values,
        up_values,
        cotangent,
        down_weight,
        up_entry,
        up_exit,
        down_entry,
        down_exit,
        moved,
        fisher,
    )
    return out.T


def solution(mesh):
    placed = (
        P(("groups", "dp", "fsdp"), None),
        P(("groups", "dp"), "fsdp"),
        P(("groups", "dp"), "fsdp"),
        P(("groups", "dp", "fsdp"), None),
        P("fsdp", "dp"),
        P(),
        P(None, "fsdp"),
        P(None, "fsdp"),
        P(),
        P("dp", None, "fsdp"),
        P(None, "fsdp", "dp"),
    )
    return jax.shard_map(
        functools.partial(local, (mesh.shape["dp"], mesh.shape["fsdp"])),
        mesh=mesh,
        in_specs=placed,
        out_specs=P(("dp", "fsdp"), "groups"),
        check_vma=False,
    )
```
